32 devices in a mesh: grp: 1, row: 1, fs: 32 (over z, y, x, core).
Axes of the slice: x: 2, y: 2, z: 4, core: 2. Of those that a mesh axis runs over, the one named last changes fastest.
Arguments:
- traces: bfloat16 [128, 512, 1024], P(('row', 'fs')), may hold values from -6 to 6
- freq_bins: int32 [4], P('grp'), may hold values from 1 to 255
- obliquity: float32 [4, 8192], P('grp'), may hold values from 0.5 to 2
- pattern: int32 [1, 8], replicated, may hold values from 0 to 63, as said below
- block_mask: int32 [1, 8], replicated, may hold values 0 or 1
- shot_bins: int32 [1, 128], replicated, may hold values from 0 to 127, each once within a row
- wavefield: bfloat16 [8192, 2, 4096], P('row', None, ('grp', 'fs')), may hold values from -0.1875 to 0.1875
Outputs:
- multiples: bfloat16 [128, 2, 4096], P('row', None, ('grp', 'fs'))
The draws below stay inside these ranges and needn't reach their ends.
Inputs may be any that keep to these rules, and one draw needn't show every extreme that they name: `pattern`: the 8 entries of a row name different receiver patches. `shot_bins`: each row is a permutation of 0 to 127.
All inputs are finite; a program needn't handle non-finite values.
Results may differ from the reference program's by a relative error of at most 0.0058.
Values may be sent and summed in bfloat16 or wider, within the bound.
A program may use at most 128 MiB of HBM per device.

```python
import math
import jax
import jax.numpy as jnp
from jax import lax

PATCH = 128
RP = 64
LIVE = 8
NT = 512
NF = 4
K = 8192
C = 1024
SHOTS = 128
SP = 1
NB = 1024


def draw_pattern(key, part):
    key = jax.random.fold_in(key, 11)
    row_keys = jax.random.split(key, SP)
    rows = jax.vmap(lambda one_key: jax.random.permutation(one_key, RP)[:LIVE])(row_keys)
    middle = jax.random.permutation(jax.random.fold_in(key, 5), RP - 2) + 1
    ends = jnp.array([0, RP - 1], dtype=middle.dtype)
    first_row = jnp.concatenate([ends, middle])[:LIVE]
    rows = rows.at[0].set(first_row)
    return rows.astype(jnp.int32)


def touch_ends(drawn, key, low, largest):
    index_at = [jax.random.randint(jax.random.fold_in(key, axis), (), 0, length) for axis, length in enumerate(drawn.shape)]
    longest = drawn.shape.index(max(drawn.shape))
    beside = index_at[:longest] + [(index_at[longest] + 1) % drawn.shape[longest]] + index_at[longest + 1:]
    return drawn.at[tuple(index_at)].set(low).at[tuple(beside)].set(largest)


def block_scale(own_key, shape, pieces, smallest, top_value):
    def one(position, parts):
        steps = jax.random.uniform(jax.random.fold_in(jax.random.fold_in(own_key, 6), position), (parts,), jnp.float32, smallest / len(pieces), top_value / len(pieces))
        return jnp.repeat(jnp.exp(steps), shape[position] // parts).reshape((-1,) + (1,) * (len(shape) - position - 1))

    gain = one(*pieces[0])
    for cut in pieces[1:]:
        gain = gain * one(*cut)
    return gain


def scatter_about(key, dims, deviation, reach, cuts=(), kind=jnp.bfloat16):
    factor_of = block_scale(key, dims, cuts, -0.22, 0.18) if cuts else 1.0
    drawn = jax.random.normal(key, dims, jnp.float32) * deviation * factor_of
    return jnp.minimum(jnp.maximum(drawn, -reach), reach).astype(kind)


def setup_inputs(seed: int = 0, part: int = 0) -> dict:
    keys = jax.random.split(jax.random.key(seed), 8)
    part_keys = jax.random.split(jax.random.fold_in(keys[7], part), 8)
    return {
        "traces": scatter_about(keys[0], (SHOTS, NT, C), 1.0, 6.0, ((0, 32),)),
        "freq_bins": touch_ends(jax.random.randint(part_keys[1], (NF,), 1, NT // 2), jax.random.fold_in(part_keys[1], 1), 1, (NT // 2) - 1).astype(jnp.int32),
        "obliquity": jnp.clip(jnp.exp(jax.random.uniform(part_keys[2], (NF, K), jnp.float32, math.log(0.5), math.log(2.0))), 0.5, 2.0),
        "pattern": draw_pattern(jax.random.fold_in(keys[7], 71), part),
        "block_mask": touch_ends((jax.random.randint(keys[4], (SP, LIVE), 0, 4) < 3).astype(jnp.int32), jax.random.fold_in(keys[4], 1), 0, 1),
        "shot_bins": jax.vmap(lambda own: jax.random.permutation(own, PATCH))(jax.random.split(keys[5], SP)).reshape((SP, PATCH)).astype(jnp.int32),
        "wavefield": scatter_about(part_keys[6], (K, 2, NF * NB), C ** -0.5, 0.1875, ((2, 32),)),
    }


def dft_rows(freq_bins):
    sample_ids = jnp.arange(NT, dtype=jnp.int32)
    wrapped = freq_bins[:, None] * sample_ids[None, :] % NT
    angles = wrapped.astype(jnp.float32) * (2.0 * math.pi / NT)
    stacked = jnp.stack([jnp.cos(angles), -jnp.sin(angles)], axis=1)
    return (stacked.reshape(2 * NF, NT) * (1.0 / math.sqrt(NT))).astype(jnp.bfloat16)

def reference(traces, freq_bins, obliquity, pattern, block_mask, shot_bins, wavefield):
    dft_table = dft_rows(freq_bins)
    spectra = lax.map(lambda one_shot: jnp.dot(dft_table, one_shot, preferred_element_type=jnp.float32), traces)
    point_ids = (pattern[:, :, None] * PATCH + jnp.arange(PATCH, dtype=jnp.int32)[None, None, :]).reshape(SP, C)
    obl_weight = jnp.transpose(obliquity[:, point_ids], (1, 0, 2))
    live_mask = jnp.repeat(block_mask, PATCH, axis=1).astype(jnp.float32)
    scaled = spectra.reshape(SP, PATCH, NF, 2, C) * obl_weight[:, None, :, None, :] * live_mask[:, None, None, None, :]
    weighted = scaled.astype(jnp.bfloat16).reshape(SHOTS, NF, 2, C)
    shot_order = (jnp.arange(SP, dtype=jnp.int32)[:, None] * PATCH + shot_bins).reshape(SHOTS)
    sorted_rows = weighted[shot_order].reshape(SP, PATCH, NF, 2, C)
    fields = wavefield.reshape(K, 2, NF, NB)

    def one_block(index):
        patch_index = index // NF
        freq_index = index % NF
        patch_rows = lax.dynamic_index_in_dim(sorted_rows, patch_index, 0, keepdims=False)
        freq_rows = lax.dynamic_index_in_dim(patch_rows, freq_index, 1, keepdims=False)
        operand = freq_rows.reshape(PATCH, 2 * C)
        freq_field = lax.dynamic_index_in_dim(fields, freq_index, 2, keepdims=False)
        patch_points = lax.dynamic_index_in_dim(point_ids, patch_index, 0, keepdims=False)
        chosen = freq_field[patch_points]
        real_part = chosen[:, 0, :]
        imag_part = chosen[:, 1, :]
        upper = jnp.concatenate([real_part, imag_part], axis=1)
        lower = jnp.concatenate([-imag_part, real_part], axis=1)
        stacked = jnp.concatenate([upper, lower], axis=0)
        return jnp.dot(operand, stacked, preferred_element_type=jnp.float32)
    blocks = lax.map(one_block, jnp.arange(SP * NF, dtype=jnp.int32))
    blocks = blocks.reshape(SP, NF, PATCH, 2, NB)
    result = jnp.transpose(blocks, (0, 2, 3, 1, 4)).reshape(SHOTS, 2, NF * NB)
    return result.astype(jnp.bfloat16)
```

```python
import functools
import math

import jax
import jax.numpy as jnp
from jax import lax
from jax.experimental import pallas as pl
from jax.experimental.pallas import tpu as pltpu
from jax.sharding import PartitionSpec as P


def dot(left, right):
    return jnp.dot(left, right, preferred_element_type=jnp.float32)


def iota(shape, axis):
    return lax.broadcasted_iota(jnp.int32, shape, axis)


def dft_rows(freq_ref, nfreq, shots, samples):
    shape = (nfreq * 2 * shots, samples)
    row = iota(shape, 0)
    freq = jnp.zeros(shape, jnp.int32)
    for f in range(nfreq):
        freq = jnp.where(lax.div(row, 2 * shots) == f, freq_ref[f], freq)
    quarter = lax.rem(lax.div(row, shots), 2) * (samples // 4)
    wrapped = (freq * iota(shape, 1) + quarter) & (samples - 1)
    folded = jnp.abs(wrapped - samples // 2) - samples // 4
    angles = folded.astype(jnp.float32) * (2.0 * math.pi / samples)
    return jnp.sin(angles) * (1.0 / math.sqrt(samples))


def kernel(
    nfs,
    nfreq,
    half_patches,
    freq_ref,
    pattern_ref,
    mask_ref,
    bins_ref,
    obl_hbm,
    traces_hbm,
    field_hbm,
    out_ref,
    obl,
    traces,
    field,
    table,
    staged,
    arrived,
    gathered,
    chosen,
    order,
    load_sem,
    send1,
    recv1,
    send2,
    recv2,
):
    shots, samples, channels = traces.shape
    blocks = pattern_ref.shape[1]
    patch = channels // blocks
    group = nfs // nfreq
    pair = 2 * shots
    half = channels // 2
    rows = group * nfreq * pair
    me = lax.axis_index("fs")
    mine, member = lax.div(me, group), lax.rem(me, group)
    patch_id = lax.axis_index("row") * half_patches + lax.div(me * shots, patch)

    loads = [pltpu.make_async_copy(obl_hbm, obl, load_sem.at[0])]
    for s in range(shots):
        loads.append(
            pltpu.make_async_copy(traces_hbm.at[s], traces.at[s], load_sem.at[1 + s])
        )
    loads.append(pltpu.make_async_copy(field_hbm, field, load_sem.at[1 + shots]))
    for load in loads:
        load.start()

    def same_member(k):
        return lax.rem(mine + k, nfreq)

    def same_group(k):
        return mine * group + lax.rem(member + k, group)

    barrier = pltpu.get_barrier_semaphore()
    for k in range(1, nfreq):
        pl.semaphore_signal(
            barrier,
            inc=1,
            device_id={"fs": same_member(k) * group + member},
            device_id_type=pl.DeviceIdType.MESH,
        )
    for k in range(1, group):
        pl.semaphore_signal(
            barrier,
            inc=1,
            device_id={"fs": same_group(k)},
            device_id_type=pl.DeviceIdType.MESH,
        )

    rows_table = dft_rows(freq_ref, nfreq, shots, samples)
    owner = lax.rem(iota(rows_table.shape, 0), shots)
    for s in range(shots):
        table[:, s * samples : (s + 1) * samples] = jnp.where(
            owner == s, rows_table, 0.0
        ).astype(jnp.bfloat16)

    for a in range(half_patches):
        bins = bins_ref[pl.ds(lax.axis_index("row") * half_patches + a, 1), :]
        shot = bins + a * patch
        device = lax.div(shot, shots)
        place = (
            lax.rem(device, group) * (nfreq * pair)
            + lax.div(device, group) * pair
            + lax.rem(shot, shots)
        )
        hot = jnp.where(iota((rows, patch), 0) == place, 1.0, 0.0).astype(jnp.bfloat16)
        for j in range(2):
            spread = jnp.where(
                iota((2 * patch, patch), 0) == 2 * iota((2 * patch, patch), 1) + j, 1.0, 0.0
            ).astype(jnp.bfloat16)
            order[a, :, j * rows : (j + 1) * rows] = lax.dot_general(
                spread, hot, (((1,), (1,)), ((), ())), preferred_element_type=jnp.float32
            ).astype(jnp.bfloat16)

    loads[0].wait()
    weights = []
    for b in range(blocks):
        live = mask_ref[patch_id, b].astype(jnp.float32)
        weights.append(obl[pattern_ref[patch_id, b]] * live)
    weights = jnp.concatenate(weights, axis=1)

    spectra = jnp.zeros((nfreq * pair, channels), jnp.float32)
    for s in range(shots):
        loads[1 + s].wait()
        spectra += dot(table[:, s * samples : (s + 1) * samples], traces[s])
    for f in range(nfreq):
        scaled = spectra[f * pair : (f + 1) * pair] * weights[f : f + 1]
        staged[f] = jnp.concatenate([scaled[:, :half], scaled[:, half:]], axis=0).astype(
            jnp.bfloat16
        )
    pl.semaphore_wait(barrier, nfreq - 1 + group - 1)

    first = []
    for k in range(1, nfreq):
        copy = pltpu.make_async_remote_copy(
            src_ref=staged.at[same_member(k)],
            dst_ref=arrived.at[mine],
            send_sem=send1.at[k - 1],
            recv_sem=recv1.at[k - 1],
            device_id={"fs": same_member(k) * group + member},
            device_id_type=pl.DeviceIdType.MESH,
        )
        copy.start()
        first.append(copy)
    arrived[mine] = staged[mine]

    loads[1 + shots].wait()
    spot = iota((2 * patch, 2 * patch), 0)
    source = jnp.where(spot < patch, 2 * spot, 2 * (spot - patch) + 1)
    split = jnp.where(iota((2 * patch, 2 * patch), 1) == source, 1.0, 0.0).astype(jnp.bfloat16)
    for a in range(half_patches):
        for b in range(blocks):
            block = pattern_ref[lax.axis_index("row") * half_patches + a, b]
            parts = dot(split, field[block]).astype(jnp.bfloat16)
            width = parts.shape[1]
            chosen[a, b * patch : (b + 1) * patch, :width] = parts[:patch]
            chosen[a, b * patch : (b + 1) * patch, width:] = parts[patch:]

    for copy in first:
        copy.wait_recv()
    pieces = []
    for z in range(nfreq):
        piece = arrived[z].astype(jnp.float32)
        pieces.append(jnp.concatenate([piece[:pair], piece[pair:]], axis=1))
    gathered[member] = jnp.concatenate(pieces, axis=0).astype(jnp.bfloat16)

    second = []
    for k in range(1, group):
        copy = pltpu.make_async_remote_copy(
            src_ref=gathered.at[member],
            dst_ref=gathered.at[member],
            send_sem=send2.at[k - 1],
            recv_sem=recv2.at[k - 1],
            device_id={"fs": same_group(k)},
            device_id_type=pl.DeviceIdType.MESH,
        )
        copy.start()
        second.append(copy)
    for copy in second:
        copy.wait_recv()

    width = field.shape[2]
    left = gathered[...].reshape(rows, channels)
    for a in range(half_patches):
        product = dot(left, chosen[a])
        by_real, by_imag = product[:, :width], product[:, width:]
        real = by_real - pltpu.roll(by_imag, rows - shots, 0)
        imag = by_imag + pltpu.roll(by_real, rows - shots, 0)
        both = jnp.concatenate([real, imag], axis=0).astype(jnp.bfloat16)
        out_ref[a * 2 * patch : (a + 1) * 2 * patch, :] = dot(order[a], both).astype(
            jnp.bfloat16
        )
    for copy in first + second:
        copy.wait_send()


def on_device(traces, freq_bins, obliquity, pattern, block_mask, shot_bins, wavefield):
    shots, samples, channels = traces.shape
    nfreq = freq_bins.shape[0]
    patch = shot_bins.shape[1]
    nfs = lax.axis_size("fs")
    group = nfs // nfreq
    half_patches = shots * nfs // patch
    columns = wavefield.shape[2]
    if lax.axis_size("row") > 1:
        wavefield = lax.all_gather(wavefield, "row", axis=0, tiled=True)
    points = wavefield.shape[0]
    rows = group * nfreq * 2 * shots
    smem = pl.BlockSpec(memory_space=pltpu.SMEM)
    vmem = pl.BlockSpec(memory_space=pltpu.VMEM)
    hbm = pl.BlockSpec(memory_space=pl.ANY)
    result = pl.pallas_call(
        functools.partial(kernel, nfs, nfreq, half_patches),
        out_shape=jax.ShapeDtypeStruct((half_patches * patch * 2, columns), jnp.bfloat16),
        in_specs=[smem, smem, smem, vmem, hbm, hbm, hbm],
        out_specs=vmem,
        scratch_shapes=[
            pltpu.VMEM((points // patch, nfreq, patch), jnp.float32),
            pltpu.VMEM(traces.shape, jnp.bfloat16),
            pltpu.VMEM((points // patch, 2 * patch, columns), jnp.bfloat16),
            pltpu.VMEM((nfreq * 2 * shots, shots * samples), jnp.bfloat16),
            pltpu.VMEM((nfreq, 4 * shots, channels // 2), jnp.bfloat16),
            pltpu.VMEM((nfreq, 4 * shots, channels // 2), jnp.bfloat16),
            pltpu.VMEM((group, nfreq * 2 * shots, channels), jnp.bfloat16),
            pltpu.VMEM((half_patches, channels, 2 * columns), jnp.bfloat16),
            pltpu.VMEM((half_patches, 2 * patch, 2 * rows), jnp.bfloat16),
            pltpu.SemaphoreType.DMA((2 + shots,)),
            pltpu.SemaphoreType.DMA((nfreq - 1,)),
            pltpu.SemaphoreType.DMA((nfreq - 1,)),
            pltpu.SemaphoreType.DMA((group - 1,)),
            pltpu.SemaphoreType.DMA((group - 1,)),
        ],
        compiler_params=pltpu.CompilerParams(
            collective_id=0, has_side_effects=True, vmem_limit_bytes=60 * 1024 * 1024
        ),
    )(
        freq_bins,
        pattern,
        block_mask,
        shot_bins,
        obliquity.reshape(nfreq, points // patch, patch).transpose(1, 0, 2),
        traces,
        wavefield.reshape(points // patch, 2 * patch, columns),
    )
    return result.reshape(half_patches * patch, 2, columns)


def solution(mesh):
    in_specs = (
        P(("row", "fs"), None, None),
        P("grp"),
        P("grp", None),
        P(),
        P(),
        P(),
        P("row", None, ("grp", "fs")),
    )
    out_specs = P("row", None, ("grp", "fs"))
    return jax.shard_map(
        on_device, mesh=mesh, in_specs=in_specs, out_specs=out_specs, check_vma=False
    )
```

```python
import functools
import math

import jax
import jax.numpy as jnp
from jax import lax
from jax.experimental import pallas as pl
from jax.experimental.pallas import tpu as pltpu
from jax.sharding import PartitionSpec as P


def dot(left, right):
    return jnp.dot(left, right, preferred_element_type=jnp.float32)


def iota(shape, axis):
    return lax.broadcasted_iota(jnp.int32, shape, axis)


def dft_rows(freq_ref, nfreq, shots, samples):
    shape = (nfreq * 2 * shots, samples)
    row = iota(shape, 0)
    freq = jnp.zeros(shape, jnp.int32)
    for f in range(nfreq):
        freq = jnp.where(lax.div(row, 2 * shots) == f, freq_ref[f], freq)
    quarter = lax.rem(lax.div(row, shots), 2) * (samples // 4)
    wrapped = (freq * iota(shape, 1) + quarter) & (samples - 1)
    folded = jnp.abs(wrapped - samples // 2) - samples // 4
    angles = folded.astype(jnp.float32) * (2.0 * math.pi / samples)
    return jnp.sin(angles) * (1.0 / math.sqrt(samples))


def kernel(
    nfs,
    nfreq,
    half_patches,
    freq_ref,
    pattern_ref,
    mask_ref,
    bins_ref,
    obl_hbm,
    traces_hbm,
    field_hbm,
    out_ref,
    obl,
    traces,
    field,
    table,
    staged,
    gathered,
    chosen,
    order,
    product,
    load_sem,
    send_z,
    recv_z,
    send_chip,
    recv_chip,
    send_core,
    recv_core,
):
    shots, samples, channels = traces.shape
    blocks = pattern_ref.shape[1]
    patch = channels // blocks
    group = nfs // nfreq
    chips = group // 2
    pair = 2 * shots
    half = channels // 2
    share = group * pair
    rows = nfreq * share
    me = lax.axis_index("fs")
    mine, member = lax.div(me, group), lax.rem(me, group)
    patch_id = lax.axis_index("row") * half_patches + lax.div(me * shots, patch)

    loads = [pltpu.make_async_copy(obl_hbm, obl, load_sem.at[0])]
    for s in range(shots):
        loads.append(
            pltpu.make_async_copy(traces_hbm.at[s], traces.at[s], load_sem.at[1 + s])
        )
    loads.append(pltpu.make_async_copy(field_hbm, field, load_sem.at[1 + shots]))
    for load in loads:
        load.start()

    chip, core = lax.div(member, 2), lax.rem(member, 2)
    sibling = member + 1 - 2 * core

    def plane(k):
        return lax.rem(mine + k, nfreq)

    def other_chip(q):
        return lax.rem(chip + q, chips) * 2 + core

    def send(src, dst, send_sem, recv_sem, target):
        copy = pltpu.make_async_remote_copy(
            src_ref=src,
            dst_ref=dst,
            send_sem=send_sem,
            recv_sem=recv_sem,
            device_id={"fs": target},
            device_id_type=pl.DeviceIdType.MESH,
        )
        copy.start()
        return copy

    barrier = pltpu.get_barrier_semaphore()
    partners = [plane(k) * group + member for k in range(1, nfreq)]
    partners += [mine * group + other_chip(q) for q in range(1, chips)]
    partners += [mine * group + sibling]
    for partner in partners:
        pl.semaphore_signal(
            barrier, inc=1, device_id={"fs": partner}, device_id_type=pl.DeviceIdType.MESH
        )

    rows_table = dft_rows(freq_ref, nfreq, shots, samples)
    owner = lax.rem(iota(rows_table.shape, 0), shots)
    for s in range(shots):
        table[:, s * samples : (s + 1) * samples] = jnp.where(
            owner == s, rows_table, 0.0
        ).astype(jnp.bfloat16)

    for a in range(half_patches):
        bins = bins_ref[pl.ds(lax.axis_index("row") * half_patches + a, 1), :]
        shot = bins + a * patch
        device = lax.div(shot, shots)
        place = (
            lax.rem(mine + nfreq - lax.div(device, group), nfreq) * share
            + lax.rem(device, group) * pair
            + lax.rem(shot, shots)
        )
        hot = jnp.where(iota((rows, patch), 0) == place, 1.0, 0.0).astype(jnp.bfloat16)
        for j in range(2):
            double = jnp.where(
                iota((2 * patch, patch), 0) == 2 * iota((2 * patch, patch), 1) + j, 1.0, 0.0
            ).astype(jnp.bfloat16)
            order[a, :, j * rows : (j + 1) * rows] = lax.dot_general(
                double, hot, (((1,), (1,)), ((), ())), preferred_element_type=jnp.float32
            ).astype(jnp.bfloat16)

    loads[0].wait()
    weights = []
    for b in range(blocks):
        live = mask_ref[patch_id, b].astype(jnp.float32)
        weights.append(obl[pattern_ref[patch_id, b]] * live)
    weights = jnp.concatenate(weights, axis=1)

    spectra = jnp.zeros((nfreq * pair, channels), jnp.float32)
    for s in range(shots):
        loads[1 + s].wait()
        spectra += dot(table[:, s * samples : (s + 1) * samples], traces[s])
    for f in range(nfreq):
        scaled = spectra[f * pair : (f + 1) * pair] * weights[f : f + 1]
        staged[f] = jnp.concatenate([scaled[:, :half], scaled[:, half:]], axis=0).astype(
            jnp.bfloat16
        )
    pl.semaphore_wait(barrier, len(partners))

    by_z = [
        send(
            staged.at[plane(k)],
            gathered.at[k, member],
            send_z.at[k - 1],
            recv_z.at[k - 1],
            plane(k) * group + member,
        )
        for k in range(1, nfreq)
    ]
    gathered[0, member] = staged[mine]
    by_chip, by_core = [], []

    def spread(k):
        block = gathered.at[k, member]
        by_chip.append(
            [
                send(
                    block,
                    block,
                    send_chip.at[k, q - 1],
                    recv_chip.at[k, q - 1],
                    mine * group + other_chip(q),
                )
                for q in range(1, chips)
            ]
        )
        by_core.append(
            [
                send(
                    block,
                    block,
                    send_core.at[k, 0],
                    recv_core.at[k, 0],
                    mine * group + sibling,
                )
            ]
        )

    def forward(k):
        for q in range(1, chips):
            by_chip[k][q - 1].wait_recv()
            block = gathered.at[k, lax.rem(chip + chips - q, chips) * 2 + core]
            by_core[k].append(
                send(
                    block,
                    block,
                    send_core.at[k, q],
                    recv_core.at[k, q],
                    mine * group + sibling,
                )
            )

    spread(0)

    loads[1 + shots].wait()
    width = field.shape[2]
    spot = iota((2 * patch, 2 * patch), 0)
    source = jnp.where(spot < patch, 2 * spot, 2 * (spot - patch) + 1)
    split = jnp.where(iota((2 * patch, 2 * patch), 1) == source, 1.0, 0.0).astype(jnp.bfloat16)
    for a in range(half_patches):
        for b in range(blocks):
            block = pattern_ref[lax.axis_index("row") * half_patches + a, b]
            parts = dot(split, field[block]).astype(jnp.bfloat16)
            top = b * patch % half
            side = b * patch // half * 2 * width
            chosen[a, top : top + patch, side : side + width] = parts[:patch]
            chosen[a, top : top + patch, side + width : side + 2 * width] = parts[patch:]

    for k in range(1, nfreq):
        by_z[k - 1].wait_recv()
        spread(k)
    for k in range(nfreq):
        forward(k)
    for k in range(nfreq):
        for copy in by_core[k]:
            copy.wait_recv()
        left = gathered[k].reshape(2 * share, half)
        for a in range(half_patches):
            halves = dot(left, chosen[a]).reshape(group, 2, pair, 4 * width)
            total = (halves[:, 0, :, : 2 * width] + halves[:, 1, :, 2 * width :]).reshape(
                share, 2 * width
            )
            by_real, by_imag = total[:, :width], total[:, width:]
            real = by_real - pltpu.roll(by_imag, share - shots, 0)
            imag = by_imag + pltpu.roll(by_real, share - shots, 0)
            product[a, k * share : (k + 1) * share] = real.astype(jnp.bfloat16)
            product[a, rows + k * share : rows + (k + 1) * share] = imag.astype(jnp.bfloat16)
    for a in range(half_patches):
        out_ref[a * 2 * patch : (a + 1) * 2 * patch, :] = dot(order[a], product[a]).astype(
            jnp.bfloat16
        )
    for copy in by_z + sum(by_chip, []) + sum(by_core, []):
        copy.wait_send()


def on_device(traces, freq_bins, obliquity, pattern, block_mask, shot_bins, wavefield):
    shots, samples, channels = traces.shape
    nfreq = freq_bins.shape[0]
    patch = shot_bins.shape[1]
    nfs = lax.axis_size("fs")
    group = nfs // nfreq
    half_patches = shots * nfs // patch
    columns = wavefield.shape[2]
    if lax.axis_size("row") > 1:
        wavefield = lax.all_gather(wavefield, "row", axis=0, tiled=True)
    points = wavefield.shape[0]
    rows = group * nfreq * 2 * shots
    smem = pl.BlockSpec(memory_space=pltpu.SMEM)
    vmem = pl.BlockSpec(memory_space=pltpu.VMEM)
    hbm = pl.BlockSpec(memory_space=pl.ANY)
    result = pl.pallas_call(
        functools.partial(kernel, nfs, nfreq, half_patches),
        out_shape=jax.ShapeDtypeStruct((half_patches * patch * 2, columns), jnp.bfloat16),
        in_specs=[smem, smem, smem, vmem, hbm, hbm, hbm],
        out_specs=vmem,
        scratch_shapes=[
            pltpu.VMEM((points // patch, nfreq, patch), jnp.float32),
            pltpu.VMEM(traces.shape, jnp.bfloat16),
            pltpu.VMEM((points // patch, 2 * patch, columns), jnp.bfloat16),
            pltpu.VMEM((nfreq * 2 * shots, shots * samples), jnp.bfloat16),
            pltpu.VMEM((nfreq, 4 * shots, channels // 2), jnp.bfloat16),
            pltpu.VMEM((nfreq, group, 4 * shots, channels // 2), jnp.bfloat16),
            pltpu.VMEM((half_patches, channels // 2, 4 * columns), jnp.bfloat16),
            pltpu.VMEM((half_patches, 2 * patch, 2 * rows), jnp.bfloat16),
            pltpu.VMEM((half_patches, 2 * rows, columns), jnp.bfloat16),
            pltpu.SemaphoreType.DMA((2 + shots,)),
            pltpu.SemaphoreType.DMA((nfreq - 1,)),
            pltpu.SemaphoreType.DMA((nfreq - 1,)),
            pltpu.SemaphoreType.DMA((nfreq, group // 2 - 1)),
            pltpu.SemaphoreType.DMA((nfreq, group // 2 - 1)),
            pltpu.SemaphoreType.DMA((nfreq, group // 2)),
            pltpu.SemaphoreType.DMA((nfreq, group // 2)),
        ],
        compiler_params=pltpu.CompilerParams(
            collective_id=0, has_side_effects=True, vmem_limit_bytes=60 * 1024 * 1024
        ),
    )(
        freq_bins,
        pattern,
        block_mask,
        shot_bins,
        obliquity.reshape(nfreq, points // patch, patch).transpose(1, 0, 2),
        traces,
        wavefield.reshape(points // patch, 2 * patch, columns),
    )
    return result.reshape(half_patches * patch, 2, columns)


def solution(mesh):
    in_specs = (
        P(("row", "fs"), None, None),
        P("grp"),
        P("grp", None),
        P(),
        P(),
        P(),
        P("row", None, ("grp", "fs")),
    )
    out_specs = P("row", None, ("grp", "fs"))
    return jax.shard_map(
        on_device, mesh=mesh, in_specs=in_specs, out_specs=out_specs, check_vma=False
    )
```

```python
import functools
import math

import jax
import jax.numpy as jnp
from jax import lax
from jax.experimental import pallas as pl
from jax.experimental.pallas import tpu as pltpu
from jax.sharding import PartitionSpec as P


def dot(left, right):
    return jnp.dot(left, right, preferred_element_type=jnp.float32)


def iota(shape, axis):
    return lax.broadcasted_iota(jnp.int32, shape, axis)


def dft_rows(freq_ref, nfreq, shots, samples):
    shape = (nfreq * 2 * shots, samples)
    row = iota(shape, 0)
    freq = jnp.zeros(shape, jnp.int32)
    for f in range(nfreq):
        freq = jnp.where(lax.div(row, 2 * shots) == f, freq_ref[f], freq)
    quarter = lax.rem(lax.div(row, shots), 2) * (samples // 4)
    wrapped = (freq * iota(shape, 1) + quarter) & (samples - 1)
    folded = jnp.abs(wrapped - samples // 2) - samples // 4
    angles = folded.astype(jnp.float32) * (2.0 * math.pi / samples)
    return jnp.sin(angles) * (1.0 / math.sqrt(samples))


def kernel(
    nfs,
    nfreq,
    half_patches,
    freq_hbm,
    pattern_hbm,
    mask_hbm,
    bins_hbm,
    obl_hbm,
    traces_hbm,
    field_hbm,
    out_ref,
    freq_ref,
    pattern_ref,
    mask_ref,
    bins_ref,
    obl,
    traces,
    field,
    table,
    staged,
    gathered,
    chosen,
    order,
    product,
    load_sem,
    send_z,
    recv_z,
    send_chip,
    recv_chip,
    send_core,
    recv_core,
):
    shots, samples, channels = traces.shape
    blocks = pattern_ref.shape[1]
    patch = channels // blocks
    group = nfs // nfreq
    chips = group // 2
    pair = 2 * shots
    half = channels // 2
    share = group * pair
    rows = nfreq * share
    me = lax.axis_index("fs")
    mine, member = lax.div(me, group), lax.rem(me, group)
    patch_id = lax.axis_index("row") * half_patches + lax.div(me * shots, patch)

    chip, core = lax.div(member, 2), lax.rem(member, 2)
    sibling = member + 1 - 2 * core

    def plane(k):
        return lax.rem(mine + k, nfreq)

    def other_chip(q):
        return lax.rem(chip + q, chips) * 2 + core

    def send(src, dst, send_sem, recv_sem, target):
        copy = pltpu.make_async_remote_copy(
            src_ref=src,
            dst_ref=dst,
            send_sem=send_sem,
            recv_sem=recv_sem,
            device_id={"fs": target},
            device_id_type=pl.DeviceIdType.MESH,
        )
        copy.start()
        return copy

    barrier = pltpu.get_barrier_semaphore()
    partners = [plane(k) * group + member for k in range(1, nfreq)]
    partners += [mine * group + other_chip(q) for q in range(1, chips)]
    partners += [mine * group + sibling]
    for partner in partners:
        pl.semaphore_signal(
            barrier, inc=1, device_id={"fs": partner}, device_id_type=pl.DeviceIdType.MESH
        )

    def load(src, dst, index):
        copy = pltpu.make_async_copy(src, dst, load_sem.at[index])
        copy.start()
        return copy

    get_freq = load(freq_hbm, freq_ref, 0)
    get_traces = [load(traces_hbm.at[s], traces.at[s], 6 + s) for s in range(shots)]
    get_pattern = load(pattern_hbm, pattern_ref, 1)
    get_mask = load(mask_hbm, mask_ref, 2)
    get_obl = load(obl_hbm, obl, 3)
    get_bins = load(bins_hbm, bins_ref, 4)
    get_field = load(field_hbm, field, 5)

    get_freq.wait()
    rows_table = dft_rows(freq_ref, nfreq, shots, samples)
    owner = lax.rem(iota(rows_table.shape, 0), shots)
    for s in range(shots):
        table[:, s * samples : (s + 1) * samples] = jnp.where(
            owner == s, rows_table, 0.0
        ).astype(jnp.bfloat16)

    get_bins.wait()
    for a in range(half_patches):
        bins = bins_ref[pl.ds(lax.axis_index("row") * half_patches + a, 1), :]
        shot = bins + a * patch
        device = lax.div(shot, shots)
        source = lax.div(device, group)
        slot = jnp.where(source < mine, source + 1, jnp.where(source == mine, 0, source))
        place = (
            slot * share
            + lax.rem(device, group) * pair
            + lax.rem(shot, shots)
        )
        hot = jnp.where(iota((rows, patch), 0) == place, 1.0, 0.0).astype(jnp.bfloat16)
        for j in range(2):
            double = jnp.where(
                iota((2 * patch, patch), 0) == 2 * iota((2 * patch, patch), 1) + j, 1.0, 0.0
            ).astype(jnp.bfloat16)
            order[a, :, j * rows : (j + 1) * rows] = lax.dot_general(
                double, hot, (((1,), (1,)), ((), ())), preferred_element_type=jnp.float32
            ).astype(jnp.bfloat16)

    get_pattern.wait()
    get_mask.wait()
    get_obl.wait()
    weights = []
    for b in range(blocks):
        live = mask_ref[patch_id, b].astype(jnp.float32)
        weights.append(obl[pattern_ref[patch_id, b]] * live)
    weights = jnp.concatenate(weights, axis=1)

    spectra = jnp.zeros((nfreq * pair, channels), jnp.float32)
    for s in range(shots):
        get_traces[s].wait()
        spectra += dot(table[:, s * samples : (s + 1) * samples], traces[s])
    for f in range(nfreq):
        scaled = spectra[f * pair : (f + 1) * pair] * weights[f : f + 1]
        staged[f] = jnp.concatenate([scaled[:, :half], scaled[:, half:]], axis=0).astype(
            jnp.bfloat16
        )
    pl.semaphore_wait(barrier, len(partners))

    by_z = []
    for k in range(1, nfreq):
        target = plane(k)
        slot = mine + 1 - lax.div(mine + nfreq - target, nfreq)
        by_z.append(
            send(
                staged.at[target],
                gathered.at[slot, member],
                send_z.at[k - 1],
                recv_z.at[slot - 1],
                target * group + member,
            )
        )
    gathered[0, member] = staged[mine]
    by_chip, by_core = [], []

    def spread(k):
        block = gathered.at[k, member]
        by_chip.append(
            [
                send(
                    block,
                    block,
                    send_chip.at[k, q - 1],
                    recv_chip.at[k, q - 1],
                    mine * group + other_chip(q),
                )
                for q in range(1, chips)
            ]
        )
        by_core.append(
            [
                send(
                    block,
                    block,
                    send_core.at[k, 0],
                    recv_core.at[k, 0],
                    mine * group + sibling,
                )
            ]
        )

    def forward(k):
        for q in range(1, chips):
            by_chip[k][q - 1].wait_recv()
            block = gathered.at[k, lax.rem(chip + chips - q, chips) * 2 + core]
            by_core[k].append(
                send(
                    block,
                    block,
                    send_core.at[k, q],
                    recv_core.at[k, q],
                    mine * group + sibling,
                )
            )

    spread(0)

    for k in range(1, nfreq):
        block = gathered.at[k, member]
        pltpu.make_async_remote_copy(
            src_ref=block,
            dst_ref=block,
            send_sem=send_z.at[k - 1],
            recv_sem=recv_z.at[k - 1],
            device_id={"fs": plane(k) * group + member},
            device_id_type=pl.DeviceIdType.MESH,
        ).wait_recv()
        spread(k)

    get_field.wait()
    width = field.shape[2]
    spot = iota((2 * patch, 2 * patch), 0)
    source = jnp.where(spot < patch, 2 * spot, 2 * (spot - patch) + 1)
    split = jnp.where(iota((2 * patch, 2 * patch), 1) == source, 1.0, 0.0).astype(jnp.bfloat16)
    for a in range(half_patches):
        for b in range(blocks):
            block = pattern_ref[lax.axis_index("row") * half_patches + a, b]
            parts = dot(split, field[block]).astype(jnp.bfloat16)
            top = b * patch % half
            side = b * patch // half * 2 * width
            chosen[a, top : top + patch, side : side + width] = parts[:patch]
            chosen[a, top : top + patch, side + width : side + 2 * width] = parts[patch:]

    for k in range(nfreq):
        forward(k)
    for k in range(nfreq):
        for copy in by_core[k]:
            copy.wait_recv()
        left = gathered[k].reshape(2 * share, half)
        for a in range(half_patches):
            halves = dot(left, chosen[a]).reshape(group, 2, pair, 4 * width)
            total = (halves[:, 0, :, : 2 * width] + halves[:, 1, :, 2 * width :]).reshape(
                share, 2 * width
            )
            by_real, by_imag = total[:, :width], total[:, width:]
            real = by_real - pltpu.roll(by_imag, share - shots, 0)
            imag = by_imag + pltpu.roll(by_real, share - shots, 0)
            product[a, k * share : (k + 1) * share] = real.astype(jnp.bfloat16)
            product[a, rows + k * share : rows + (k + 1) * share] = imag.astype(jnp.bfloat16)
    for a in range(half_patches):
        out_ref[a * 2 * patch : (a + 1) * 2 * patch, :] = dot(order[a], product[a]).astype(
            jnp.bfloat16
        )
    for copy in by_z + sum(by_chip, []) + sum(by_core, []):
        copy.wait_send()


def on_device(traces, freq_bins, obliquity, pattern, block_mask, shot_bins, wavefield):
    shots, samples, channels = traces.shape
    nfreq = freq_bins.shape[0]
    patch = shot_bins.shape[1]
    nfs = lax.axis_size("fs")
    group = nfs // nfreq
    half_patches = shots * nfs // patch
    columns = wavefield.shape[2]
    if lax.axis_size("row") > 1:
        wavefield = lax.all_gather(wavefield, "row", axis=0, tiled=True)
    points = wavefield.shape[0]
    rows = group * nfreq * 2 * shots
    vmem = pl.BlockSpec(memory_space=pltpu.VMEM)
    hbm = pl.BlockSpec(memory_space=pl.ANY)
    result = pl.pallas_call(
        functools.partial(kernel, nfs, nfreq, half_patches),
        out_shape=jax.ShapeDtypeStruct((half_patches * patch * 2, columns), jnp.bfloat16),
        in_specs=[hbm] * 7,
        out_specs=vmem,
        scratch_shapes=[
            pltpu.SMEM(freq_bins.shape, jnp.int32),
            pltpu.SMEM(pattern.shape, jnp.int32),
            pltpu.SMEM(block_mask.shape, jnp.int32),
            pltpu.VMEM(shot_bins.shape, jnp.int32),
            pltpu.VMEM((points // patch, nfreq, patch), jnp.float32),
            pltpu.VMEM(traces.shape, jnp.bfloat16),
            pltpu.VMEM((points // patch, 2 * patch, columns), jnp.bfloat16),
            pltpu.VMEM((nfreq * 2 * shots, shots * samples), jnp.bfloat16),
            pltpu.VMEM((nfreq, 4 * shots, channels // 2), jnp.bfloat16),
            pltpu.VMEM((nfreq, group, 4 * shots, channels // 2), jnp.bfloat16),
            pltpu.VMEM((half_patches, channels // 2, 4 * columns), jnp.bfloat16),
            pltpu.VMEM((half_patches, 2 * patch, 2 * rows), jnp.bfloat16),
            pltpu.VMEM((half_patches, 2 * rows, columns), jnp.bfloat16),
            pltpu.SemaphoreType.DMA((6 + shots,)),
            pltpu.SemaphoreType.DMA((nfreq - 1,)),
            pltpu.SemaphoreType.DMA((nfreq - 1,)),
            pltpu.SemaphoreType.DMA((nfreq, group // 2 - 1)),
            pltpu.SemaphoreType.DMA((nfreq, group // 2 - 1)),
            pltpu.SemaphoreType.DMA((nfreq, group // 2)),
            pltpu.SemaphoreType.DMA((nfreq, group // 2)),
        ],
        compiler_params=pltpu.CompilerParams(
            collective_id=0, has_side_effects=True, vmem_limit_bytes=60 * 1024 * 1024
        ),
    )(
        freq_bins,
        pattern,
        block_mask,
        shot_bins,
        obliquity.reshape(nfreq, points // patch, patch).transpose(1, 0, 2),
        traces,
        wavefield.reshape(points // patch, 2 * patch, columns),
    )
    return result.reshape(half_patches * patch, 2, columns)


def solution(mesh):
    in_specs = (
        P(("row", "fs"), None, None),
        P("grp"),
        P("grp", None),
        P(),
        P(),
        P(),
        P("row", None, ("grp", "fs")),
    )
    out_specs = P("row", None, ("grp", "fs"))
    return jax.shard_map(
        on_device, mesh=mesh, in_specs=in_specs, out_specs=out_specs, check_vma=False
    )
```

```python
import functools
import math

import jax
import jax.numpy as jnp
from jax import lax
from jax.experimental import pallas as pl
from jax.experimental.pallas import tpu as pltpu
from jax.sharding import PartitionSpec as P


def dot(left, right):
    return jnp.dot(left, right, preferred_element_type=jnp.float32)


def iota(shape, axis):
    return lax.broadcasted_iota(jnp.int32, shape, axis)


def dft_rows(freq_ref, nfreq, shots, samples):
    shape = (nfreq * 2 * shots, samples)
    row = iota(shape, 0)
    freq = jnp.zeros(shape, jnp.int32)
    for f in range(nfreq):
        freq = jnp.where(lax.div(row, 2 * shots) == f, freq_ref[f], freq)
    quarter = lax.rem(lax.div(row, shots), 2) * (samples // 4)
    wrapped = (freq * iota(shape, 1) + quarter) & (samples - 1)
    folded = jnp.abs(wrapped - samples // 2) - samples // 4
    angles = folded.astype(jnp.float32) * (2.0 * math.pi / samples)
    return jnp.sin(angles) * (1.0 / math.sqrt(samples))


def kernel(
    nfs,
    nfreq,
    half_patches,
    freq_hbm,
    pattern_hbm,
    mask_hbm,
    bins_hbm,
    obl_hbm,
    traces_hbm,
    field_hbm,
    out_ref,
    freq_ref,
    pattern_ref,
    mask_ref,
    bins_ref,
    obl,
    traces,
    field,
    table,
    staged,
    gathered,
    chosen,
    order,
    product,
    load_sem,
    send_z,
    recv_z,
    send_chip,
    recv_chip,
    send_core,
    recv_core,
):
    shots, samples, channels = traces.shape
    blocks = pattern_ref.shape[1]
    patch = channels // blocks
    group = nfs // nfreq
    chips = group // 2
    pair = 2 * shots
    half = channels // 2
    share = group * pair
    rows = nfreq * share
    me = lax.axis_index("fs")
    mine, member = lax.div(me, group), lax.rem(me, group)
    patch_id = lax.axis_index("row") * half_patches + lax.div(me * shots, patch)

    chip, core = lax.div(member, 2), lax.rem(member, 2)
    sibling = member + 1 - 2 * core

    def plane(k):
        return lax.rem(mine + k, nfreq)

    def other_chip(q):
        return lax.rem(chip + q, chips) * 2 + core

    def send(src, dst, send_sem, recv_sem, target):
        copy = pltpu.make_async_remote_copy(
            src_ref=src,
            dst_ref=dst,
            send_sem=send_sem,
            recv_sem=recv_sem,
            device_id={"fs": target},
            device_id_type=pl.DeviceIdType.MESH,
        )
        copy.start()
        return copy

    barrier = pltpu.get_barrier_semaphore()
    partners = [plane(k) * group + member for k in range(1, nfreq)]
    partners += [mine * group + other_chip(q) for q in range(1, chips)]
    partners += [mine * group + sibling]
    for partner in partners:
        pl.semaphore_signal(
            barrier, inc=1, device_id={"fs": partner}, device_id_type=pl.DeviceIdType.MESH
        )

    def load(src, dst, index):
        copy = pltpu.make_async_copy(src, dst, load_sem.at[index])
        copy.start()
        return copy

    get_freq = load(freq_hbm, freq_ref, 0)
    get_traces = [load(traces_hbm.at[s], traces.at[s], 6 + s) for s in range(shots)]
    get_pattern = load(pattern_hbm, pattern_ref, 1)
    get_mask = load(mask_hbm, mask_ref, 2)
    get_obl = load(obl_hbm, obl, 3)
    get_bins = load(bins_hbm, bins_ref, 4)
    get_field = load(field_hbm, field, 5)

    get_freq.wait()
    rows_table = dft_rows(freq_ref, nfreq, shots, samples)
    owner = lax.rem(iota(rows_table.shape, 0), shots)
    for s in range(shots):
        table[:, s * samples : (s + 1) * samples] = jnp.where(
            owner == s, rows_table, 0.0
        ).astype(jnp.bfloat16)

    get_bins.wait()
    for a in range(half_patches):
        bins = bins_ref[pl.ds(lax.axis_index("row") * half_patches + a, 1), :]
        shot = bins + a * patch
        device = lax.div(shot, shots)
        source = lax.div(device, group)
        slot = jnp.where(source < mine, source + 1, jnp.where(source == mine, 0, source))
        place = (
            slot * share
            + lax.rem(device, group) * pair
            + lax.rem(shot, shots)
        )
        hot = jnp.where(iota((rows, patch), 0) == place, 1.0, 0.0).astype(jnp.bfloat16)
        for j in range(2):
            double = jnp.where(
                iota((2 * patch, patch), 0) == 2 * iota((2 * patch, patch), 1) + j, 1.0, 0.0
            ).astype(jnp.bfloat16)
            order[a, :, j * rows : (j + 1) * rows] = lax.dot_general(
                double, hot, (((1,), (1,)), ((), ())), preferred_element_type=jnp.float32
            ).astype(jnp.bfloat16)

    get_pattern.wait()
    get_mask.wait()
    get_obl.wait()
    weights = []
    for b in range(blocks):
        live = mask_ref[patch_id, b].astype(jnp.float32)
        weights.append(obl[pattern_ref[patch_id, b]] * live)
    weights = jnp.concatenate(weights, axis=1)

    for s in range(shots):
        get_traces[s].wait()
    spectra = dot(table[...], traces[...].reshape(shots * samples, channels))
    for f in range(nfreq):
        scaled = spectra[f * pair : (f + 1) * pair] * weights[f : f + 1]
        staged[f] = jnp.concatenate([scaled[:, :half], scaled[:, half:]], axis=0).astype(
            jnp.bfloat16
        )
    pl.semaphore_wait(barrier, len(partners))

    by_z = []
    for k in range(1, nfreq):
        target = plane(k)
        slot = mine + 1 - lax.div(mine + nfreq - target, nfreq)
        by_z.append(
            send(
                staged.at[target],
                gathered.at[slot, member],
                send_z.at[k - 1],
                recv_z.at[slot - 1],
                target * group + member,
            )
        )
    gathered[0, member] = staged[mine]
    by_chip, by_core = [], []

    def spread(k):
        block = gathered.at[k, member]
        by_chip.append(
            [
                send(
                    block,
                    block,
                    send_chip.at[k, q - 1],
                    recv_chip.at[k, q - 1],
                    mine * group + other_chip(q),
                )
                for q in range(1, chips)
            ]
        )
        by_core.append(
            [
                send(
                    block,
                    block,
                    send_core.at[k, 0],
                    recv_core.at[k, 0],
                    mine * group + sibling,
                )
            ]
        )

    def forward(k):
        for q in range(1, chips):
            by_chip[k][q - 1].wait_recv()
            block = gathered.at[k, lax.rem(chip + chips - q, chips) * 2 + core]
            by_core[k].append(
                send(
                    block,
                    block,
                    send_core.at[k, q],
                    recv_core.at[k, q],
                    mine * group + sibling,
                )
            )

    spread(0)

    for k in range(1, nfreq):
        block = gathered.at[k, member]
        pltpu.make_async_remote_copy(
            src_ref=block,
            dst_ref=block,
            send_sem=send_z.at[k - 1],
            recv_sem=recv_z.at[k - 1],
            device_id={"fs": plane(k) * group + member},
            device_id_type=pl.DeviceIdType.MESH,
        ).wait_recv()
        spread(k)

    get_field.wait()
    width = field.shape[2]
    spot = iota((2 * patch, 2 * patch), 0)
    source = jnp.where(spot < patch, 2 * spot, 2 * (spot - patch) + 1)
    split = jnp.where(iota((2 * patch, 2 * patch), 1) == source, 1.0, 0.0).astype(jnp.bfloat16)
    for a in range(half_patches):
        for b in range(blocks):
            block = pattern_ref[lax.axis_index("row") * half_patches + a, b]
            parts = dot(split, field[block]).astype(jnp.bfloat16)
            top = b * patch % half
            side = b * patch // half * 2 * width
            chosen[a, top : top + patch, side : side + width] = parts[:patch]
            chosen[a, top : top + patch, side + width : side + 2 * width] = parts[patch:]

    for k in range(nfreq):
        forward(k)
    for k in range(nfreq):
        for copy in by_core[k]:
            copy.wait_recv()
        left = gathered[k].reshape(2 * share, half)
        for a in range(half_patches):
            halves = dot(left, chosen[a]).reshape(group, 2, pair, 4 * width)
            total = (halves[:, 0, :, : 2 * width] + halves[:, 1, :, 2 * width :]).reshape(
                share, 2 * width
            )
            by_real, by_imag = total[:, :width], total[:, width:]
            real = by_real - pltpu.roll(by_imag, share - shots, 0)
            imag = by_imag + pltpu.roll(by_real, share - shots, 0)
            product[a, k * share : (k + 1) * share] = real.astype(jnp.bfloat16)
            product[a, rows + k * share : rows + (k + 1) * share] = imag.astype(jnp.bfloat16)
    for a in range(half_patches):
        out_ref[a * 2 * patch : (a + 1) * 2 * patch, :] = dot(order[a], product[a]).astype(
            jnp.bfloat16
        )
    for copy in by_z + sum(by_chip, []) + sum(by_core, []):
        copy.wait_send()


def on_device(traces, freq_bins, obliquity, pattern, block_mask, shot_bins, wavefield):
    shots, samples, channels = traces.shape
    nfreq = freq_bins.shape[0]
    patch = shot_bins.shape[1]
    nfs = lax.axis_size("fs")
    group = nfs // nfreq
    half_patches = shots * nfs // patch
    columns = wavefield.shape[2]
    if lax.axis_size("row") > 1:
        wavefield = lax.all_gather(wavefield, "row", axis=0, tiled=True)
    points = wavefield.shape[0]
    rows = group * nfreq * 2 * shots
    vmem = pl.BlockSpec(memory_space=pltpu.VMEM)
    hbm = pl.BlockSpec(memory_space=pl.ANY)
    result = pl.pallas_call(
        functools.partial(kernel, nfs, nfreq, half_patches),
        out_shape=jax.ShapeDtypeStruct((half_patches * patch * 2, columns), jnp.bfloat16),
        in_specs=[hbm] * 7,
        out_specs=vmem,
        scratch_shapes=[
            pltpu.SMEM(freq_bins.shape, jnp.int32),
            pltpu.SMEM(pattern.shape, jnp.int32),
            pltpu.SMEM(block_mask.shape, jnp.int32),
            pltpu.VMEM(shot_bins.shape, jnp.int32),
            pltpu.VMEM((points // patch, nfreq, patch), jnp.float32),
            pltpu.VMEM(traces.shape, jnp.bfloat16),
            pltpu.VMEM((points // patch, 2 * patch, columns), jnp.bfloat16),
            pltpu.VMEM((nfreq * 2 * shots, shots * samples), jnp.bfloat16),
            pltpu.VMEM((nfreq, 4 * shots, channels // 2), jnp.bfloat16),
            pltpu.VMEM((nfreq, group, 4 * shots, channels // 2), jnp.bfloat16),
            pltpu.VMEM((half_patches, channels // 2, 4 * columns), jnp.bfloat16),
            pltpu.VMEM((half_patches, 2 * patch, 2 * rows), jnp.bfloat16),
            pltpu.VMEM((half_patches, 2 * rows, columns), jnp.bfloat16),
            pltpu.SemaphoreType.DMA((6 + shots,)),
            pltpu.SemaphoreType.DMA((nfreq - 1,)),
            pltpu.SemaphoreType.DMA((nfreq - 1,)),
            pltpu.SemaphoreType.DMA((nfreq, group // 2 - 1)),
            pltpu.SemaphoreType.DMA((nfreq, group // 2 - 1)),
            pltpu.SemaphoreType.DMA((nfreq, group // 2)),
            pltpu.SemaphoreType.DMA((nfreq, group // 2)),
        ],
        compiler_params=pltpu.CompilerParams(
            collective_id=0, has_side_effects=True, vmem_limit_bytes=60 * 1024 * 1024
        ),
    )(
        freq_bins,
        pattern,
        block_mask,
        shot_bins,
        obliquity.reshape(nfreq, points // patch, patch).transpose(1, 0, 2),
        traces,
        wavefield.reshape(points // patch, 2 * patch, columns),
    )
    return result.reshape(half_patches * patch, 2, columns)


def solution(mesh):
    in_specs = (
        P(("row", "fs"), None, None),
        P("grp"),
        P("grp", None),
        P(),
        P(),
        P(),
        P("row", None, ("grp", "fs")),
    )
    out_specs = P("row", None, ("grp", "fs"))
    return jax.shard_map(
        on_device, mesh=mesh, in_specs=in_specs, out_specs=out_specs, check_vma=False
    )
```
